512 devices in a mesh: dp: 16 (over z), ctx: 16 (over x, y_lo, core), track: 2 (over y_hi).
Axes of the slice: x: 4, y: 4 (y_hi: 2, y_lo: 2; y = y_hi * 2 + y_lo), z: 16, core: 2. Of those that a mesh axis runs over, the one named last changes fastest.
Arguments:
- inputs: bfloat16 [16, 2048, 768], P('dp', 'ctx'), may hold values from -40 to 40
- teacher: bfloat16 [16, 2048, 2816], P('dp', 'ctx', 'track'), may hold values from -12 to 100
- member: int32 [16], P('dp'), may hold values from 0 to 3
- member_bias: float32 [4, 2816], P(None, 'track'), may hold values from -6 to 6
- assay: int32 [2816], P('track'), may hold values from 0 to 3
- assay_temp: float32 [4], replicated, may hold values from 0.25 to 1
- conv_weight: bfloat16 [2304, 384], P('dp'), may hold values from -0.125 to 0.125
- proj_weight: bfloat16 [384, 768], P('dp'), may hold values from -0.3125 to 0.3125
- head_weight: bfloat16 [768, 2816], P('dp', 'track')
Outputs:
- grad_input: float32 [16, 2048, 768], P('dp', 'ctx')
- grad_conv: float32 [2304, 384], P(('dp', 'ctx'))
The draws below stay inside these ranges and needn't reach their ends.
All inputs are finite; a program needn't handle non-finite values.
Results may differ from the reference program's by a relative error of at most 0.0048.
Values may be sent and summed in bfloat16 or wider, within the bound.
No kernel may reach another device: no remote copies, remote signals or barrier semaphores. Data moves between devices by JAX's collectives and lax.ppermute only.
A program may use at most 64 MiB of HBM per device.

```python
import math
import jax
import jax.numpy as jnp
from jax import lax

TOWER_CHANNELS = 768
CH = 384
MEMBERS = 4
ASSAYS = 4
TRACKS = 2816
LENGTH = 2048
SEQS = 16
DILATION_SPAN = 512


def head_base(key):
    return jnp.clip(jax.random.normal(jax.random.fold_in(key, 11), (TOWER_CHANNELS, TRACKS), jnp.float32), -6.0, 6.0)


def draw_head_weight(key, part):
    base_cols = head_base(key)
    return (base_cols * TOWER_CHANNELS ** (-0.5)).astype(jnp.bfloat16)


def draw_inputs(key, part):
    key = jax.random.fold_in(key, 5)
    values = jnp.clip(jax.random.normal(key, (SEQS, LENGTH, TOWER_CHANNELS), jnp.float32), -6.0, 6.0)
    return values.astype(jnp.bfloat16)


def draw_teacher(key, part):
    key = jax.random.fold_in(key, 7)
    values = jnp.clip(3.0 * jax.random.normal(key, (SEQS, LENGTH, TRACKS), jnp.float32), -12.0, 12.0)
    return values.astype(jnp.bfloat16)


def set_ends(array, rng, least, top_value):
    place = [jax.random.randint(jax.random.fold_in(rng, axis), (), 0, length) for axis, length in enumerate(array.shape)]
    longest = array.shape.index(max(array.shape))
    neighbour = place[:longest] + [(place[longest] + 1) % array.shape[longest]] + place[longest + 1:]
    return array.at[tuple(place)].set(least).at[tuple(neighbour)].set(top_value)


def level_of(own_key, dims, cuts, low, top_value):
    loudness, own = 1.0, jax.random.fold_in(own_key, 6)
    for axis_at, blocks in cuts:
        draws = jnp.exp(jax.random.uniform(jax.random.fold_in(own, axis_at), (blocks,), jnp.float32, low / len(cuts), top_value / len(cuts)))
        loudness = loudness * jnp.repeat(draws, dims[axis_at] // blocks).reshape([-1 if axis == axis_at else 1 for axis in range(len(dims))])
    return loudness


def gaussian(own_key, dims, width, limit, pieces=(), kind=jnp.bfloat16):
    loudness = level_of(own_key, dims, pieces, -0.22, 0.18) if pieces else 1.0
    entries = jax.random.normal(own_key, dims, jnp.float32) * width * loudness
    return jnp.minimum(jnp.maximum(entries, -limit), limit).astype(kind)


def setup_inputs(seed: int = 0) -> dict:
    key_list = jax.random.split(jax.random.key(seed), 10)
    inputs = draw_inputs(jax.random.fold_in(key_list[9], 71), 0)
    teacher = draw_teacher(jax.random.fold_in(key_list[9], 71), 0)
    member = set_ends(jax.random.randint(key_list[2], (SEQS,), 0, MEMBERS), jax.random.fold_in(key_list[2], 1), 0, MEMBERS - 1).astype(jnp.int32)
    member_bias = gaussian(key_list[3], (MEMBERS, TRACKS), 1.0, 6.0, ((1, 2),), jnp.float32)
    assay = set_ends(jax.random.randint(key_list[4], (TRACKS,), 0, ASSAYS), jax.random.fold_in(key_list[4], 1), 0, ASSAYS - 1).astype(jnp.int32)
    assay_temp = jnp.clip(jnp.exp(jax.random.uniform(key_list[5], (ASSAYS,), jnp.float32, math.log(0.25), math.log(1.0))), 0.25, 1.0)
    conv_weight = gaussian(key_list[6], (3 * TOWER_CHANNELS, CH), (3 * TOWER_CHANNELS) ** -0.5, 0.125, ((0, 16),))
    proj_weight = gaussian(key_list[7], (CH, TOWER_CHANNELS), CH ** -0.5, 0.3125, ((0, 16),))
    head_weight = draw_head_weight(jax.random.fold_in(key_list[9], 71), 0)
    return dict(inputs=inputs, teacher=teacher, member=member, member_bias=member_bias, assay=assay, assay_temp=assay_temp, conv_weight=conv_weight, proj_weight=proj_weight, head_weight=head_weight)


def gelu_tanh(values):
    return jax.nn.gelu(values, approximate=True)

def displaced_row_block(values, offset):
    filler = jnp.zeros((abs(offset),) + values.shape[1:], values.dtype)
    if offset > 0:
        return jnp.concatenate([filler, values[:-offset]], axis=0)
    return jnp.concatenate([values[-offset:], filler], axis=0)

def one_sequence(sequence_row_block, teacher_rows, member_id, member_bias, temp_cols, conv_weight, proj_weight, head_weight):
    stacked_taps = jnp.concatenate([displaced_row_block(sequence_row_block, DILATION_SPAN), sequence_row_block, displaced_row_block(sequence_row_block, -DILATION_SPAN)], axis=1)
    pre_act = jnp.dot(stacked_taps, conv_weight, preferred_element_type=jnp.float32)
    gated = gelu_tanh(pre_act).astype(jnp.bfloat16)
    hidden = (sequence_row_block.astype(jnp.float32) + jnp.dot(gated, proj_weight, preferred_element_type=jnp.float32)).astype(jnp.bfloat16)
    student = jnp.dot(hidden, head_weight, preferred_element_type=jnp.float32)
    member_hit = (jnp.arange(MEMBERS, dtype=jnp.int32) == member_id).astype(jnp.float32)
    member_row = lax.optimization_barrier(jnp.sum(member_hit[:, None] * member_bias, axis=0))
    target = (teacher_rows.astype(jnp.float32) + member_row[None, :]) / temp_cols[None, :]
    q_student = jax.nn.softmax(student, axis=-1)
    p_target = jax.nn.softmax(target, axis=-1)
    logit_grad = (TRACKS * (q_student - p_target)).astype(jnp.bfloat16)
    hidden_state_gradient = jnp.dot(logit_grad, head_weight.T, preferred_element_type=jnp.float32)
    hidden_grad_b = hidden_state_gradient.astype(jnp.bfloat16)
    gated_grad = jnp.dot(hidden_grad_b, proj_weight.T, preferred_element_type=jnp.float32)
    unused, pullback = jax.vjp(gelu_tanh, pre_act)
    pre_grad = pullback(gated_grad)[0].astype(jnp.bfloat16)
    dilation_gap = jnp.dot(pre_grad, conv_weight.T, preferred_element_type=jnp.float32)
    gradient_row_block = hidden_state_gradient + displaced_row_block(dilation_gap[:, :TOWER_CHANNELS], -DILATION_SPAN) + dilation_gap[:, TOWER_CHANNELS:2 * TOWER_CHANNELS] + displaced_row_block(dilation_gap[:, 2 * TOWER_CHANNELS:], DILATION_SPAN)
    kernel_term = jnp.dot(stacked_taps.T, pre_grad, preferred_element_type=jnp.float32)
    return (gradient_row_block, kernel_term)

def reference(inputs, teacher, member, member_bias, assay, assay_temp, conv_weight, proj_weight, head_weight):
    assay_hit = (assay[:, None] == jnp.arange(ASSAYS, dtype=jnp.int32)[None, :]).astype(jnp.float32)
    temp_cols = lax.optimization_barrier(jnp.sum(assay_hit * assay_temp[None, :], axis=1))

    def step_fn(kernel_sum, bundle):
        sequence_row_block, teacher_rows, member_id = bundle
        gradient_row_block, kernel_term = one_sequence(sequence_row_block, teacher_rows, member_id, member_bias, temp_cols, conv_weight, proj_weight, head_weight)
        return (kernel_sum + kernel_term, gradient_row_block)
    kernel_zero = jnp.zeros((3 * TOWER_CHANNELS, CH), jnp.float32)
    kernel_sum, grad_input = lax.scan(step_fn, kernel_zero, (inputs, teacher, member))
    grad_conv = kernel_sum / math.sqrt(SEQS * LENGTH)
    return (grad_input, grad_conv)
```

```python
import math

import jax
import jax.numpy as jnp
from jax import lax
from jax.sharding import Mesh, PartitionSpec as P

BF = jnp.bfloat16
F32 = jnp.float32
CTX = ("x", "yl", "c")
YR = ("yl", "yh")


def gelu_tanh(values):
    return jax.nn.gelu(values, approximate=True)


def spread(value, axis):
    count = lax.axis_size(axis)
    copies = jnp.broadcast_to(value[None], (count,) + value.shape)
    return lax.all_to_all(copies, axis, 0, 0)


def shifted(value, steps):
    count = lax.axis_size("x")
    first, last = max(0, -steps), min(count, count - steps)
    return lax.ppermute(value, "x", [(s, s + steps) for s in range(first, last)])


def swapped(value, axis):
    return lax.ppermute(value, axis, [(0, 1), (1, 0)])


def rows_product(left, weight_rows):
    return lax.dot_general(
        left, weight_rows, (((1,), (1,)), ((), ())), preferred_element_type=F32
    )


def on_device(
    inputs, teacher, member, member_bias, assay, assay_temp, conv_weight, proj_weight, head_weight
):
    rows = inputs[0]
    pos, width = rows.shape
    half = pos // 2
    ch = conv_weight.shape[1]
    zc = lax.axis_size("z")
    cc = lax.axis_size(CTX)
    yh = lax.axis_index("yh")

    head_full = lax.all_gather(head_weight, "z", axis=0, tiled=True)

    rows_before = shifted(rows, 1)
    rows_after = shifted(rows, -1)

    proj_cut = proj_weight.shape[0]
    packed = jnp.concatenate([conv_weight, proj_weight[:, :ch], proj_weight[:, ch:]], axis=0)
    slab = packed.shape[0] // 8
    place = lax.axis_index(("c", "yl", "yh"))
    mine = lax.dynamic_slice_in_dim(packed, place * slab, slab, axis=0)
    over_z = spread(mine, "z")
    over_y = spread(over_z, YR).reshape(4, zc, slab, ch)
    other = swapped(over_y, "c")
    core = lax.axis_index("c")
    first = jnp.where(core == 0, over_y, other)
    second = jnp.where(core == 0, other, over_y)
    slabs = jnp.concatenate([first, second], axis=0)
    conv_slabs = conv_weight.shape[0] // slab
    conv_full = slabs[:conv_slabs].transpose(1, 0, 2, 3).reshape(zc * conv_weight.shape[0], ch)
    proj_left = slabs[conv_slabs].reshape(zc * proj_cut, ch)
    proj_right = slabs[conv_slabs + 1].reshape(zc * proj_cut, ch)
    proj_full = jnp.concatenate([proj_left, proj_right], axis=1)

    member_hit = (jnp.arange(member_bias.shape[0], dtype=jnp.int32) == member[0]).astype(F32)
    member_row = jnp.sum(member_hit[:, None] * member_bias, axis=0)
    assay_hit = (
        assay[:, None] == jnp.arange(assay_temp.shape[0], dtype=jnp.int32)[None, :]
    ).astype(F32)
    temp_cols = jnp.sum(assay_hit * assay_temp[None, :], axis=1)
    target = (teacher[0].astype(F32) + member_row[None, :]) / temp_cols[None, :]
    peak_t = jnp.max(target, axis=1)
    exp_t = jnp.exp(target - peak_t[:, None])
    sum_t = jnp.sum(exp_t, axis=1)

    stacked = jnp.concatenate([rows_before, rows, rows_after], axis=1)
    pre_act = jnp.dot(stacked, conv_full, preferred_element_type=F32)
    gated = gelu_tanh(pre_act).astype(BF)
    hidden = (rows.astype(F32) + jnp.dot(gated, proj_full, preferred_element_type=F32)).astype(BF)

    part = conv_weight.shape[0] // cc
    by_owner = stacked.T.reshape(zc, cc, part, pos).transpose(1, 0, 2, 3).reshape(cc, zc * part, pos)
    owned = lax.all_to_all(by_owner, CTX, 0, 0)
    owned = lax.dynamic_slice_in_dim(owned, yh * half, half, axis=2)
    owned = owned.transpose(1, 0, 2).reshape(zc * part, cc * half)

    student = jnp.dot(hidden, head_full, preferred_element_type=F32)
    peak_s = jnp.max(student, axis=1)
    exp_s = jnp.exp(student - peak_s[:, None])
    sum_s = jnp.sum(exp_s, axis=1)
    stats = lax.all_gather(jnp.stack([peak_s, sum_s, peak_t, sum_t]), "yh", axis=0)
    top_s = jnp.maximum(stats[0, 0], stats[1, 0])
    top_t = jnp.maximum(stats[0, 2], stats[1, 2])
    total_s = stats[0, 1] * jnp.exp(stats[0, 0] - top_s) + stats[1, 1] * jnp.exp(stats[1, 0] - top_s)
    total_t = stats[0, 3] * jnp.exp(stats[0, 2] - top_t) + stats[1, 3] * jnp.exp(stats[1, 2] - top_t)
    tracks = teacher.shape[2] * lax.axis_size("yh")
    scale_s = tracks * jnp.exp(peak_s - top_s) / total_s
    scale_t = tracks * jnp.exp(peak_t - top_t) / total_t
    logit_grad = (exp_s * scale_s[:, None] - exp_t * scale_t[:, None]).astype(BF)
    partial = rows_product(logit_grad, head_full)

    sent = lax.dynamic_slice_in_dim(partial, (1 - yh) * half, half, axis=0).astype(BF)
    kept = lax.dynamic_slice_in_dim(partial, yh * half, half, axis=0)
    hidden_grad = kept + swapped(sent, "yh").astype(F32)
    gated_grad = rows_product(hidden_grad.astype(BF), proj_full)
    unused, pullback = jax.vjp(gelu_tanh, lax.dynamic_slice_in_dim(pre_act, yh * half, half, axis=0))
    pre_grad = pullback(gated_grad)[0].astype(BF)

    grad_after = shifted(pre_grad, -1)
    grad_before = shifted(pre_grad, 1)
    everyone = lax.all_gather(pre_grad, CTX, axis=0, tiled=True)
    kernel_part = jnp.dot(owned, everyone, preferred_element_type=F32).astype(BF)
    kernel_part = kernel_part.reshape(zc, 1, part, ch)
    kernel_part = jnp.broadcast_to(kernel_part, (zc, 2, part, ch)).reshape(2 * zc, part, ch)
    terms = lax.all_to_all(kernel_part, ("z", "yh"), 0, 0)
    grad_conv = jnp.sum(terms.astype(F32), axis=0) / math.sqrt(zc * cc * pos)

    grad_rows = (
        hidden_grad
        + rows_product(grad_after, conv_full[:width])
        + rows_product(pre_grad, conv_full[width : 2 * width])
        + rows_product(grad_before, conv_full[2 * width :])
    )
    grad_other = swapped(grad_rows, "yh")
    grad_input = jnp.where(
        yh == 0,
        jnp.concatenate([grad_rows, grad_other], axis=0),
        jnp.concatenate([grad_other, grad_rows], axis=0),
    )
    return (grad_input[None], grad_conv)


def solution(mesh):
    fine = Mesh(mesh.devices.reshape(16, 4, 2, 2, 2), ("z", "x", "yl", "c", "yh"))
    return jax.shard_map(
        on_device,
        mesh=fine,
        in_specs=(
            P("z", CTX, None),
            P("z", CTX, "yh"),
            P("z"),
            P(None, "yh"),
            P("yh"),
            P(),
            P("z", None),
            P("z", None),
            P("z", "yh"),
        ),
        out_specs=(P("z", CTX, None), P(("z",) + CTX, None)),
        check_vma=False,
    )
```

```python
import functools
import math

import jax
import jax.numpy as jnp
from jax import lax
from jax.experimental import pallas as pl
from jax.experimental.pallas import tpu as pltpu
from jax.sharding import Mesh, PartitionSpec as P

BF = jnp.bfloat16
F32 = jnp.float32
CTX = ("x", "yl", "c")
YR = ("yl", "yh")
VMEM_LIMIT = 12
CURVE = 0.044715
SLOPE = math.sqrt(2.0 / math.pi)
SDS = jax.ShapeDtypeStruct


def gelu_tanh(values):
    return 0.5 * values * (1.0 + jnp.tanh(SLOPE * (values + CURVE * values * values * values)))


def gelu_slope(values):
    square = values * values
    bend = jnp.tanh(SLOPE * (values + CURVE * values * square))
    return 0.5 * (1.0 + bend) + 0.5 * values * (1.0 - bend * bend) * SLOPE * (
        1.0 + 3.0 * CURVE * square
    )


def mm(left, right):
    return jnp.dot(left, right, preferred_element_type=F32)


def mm_t(left, right_rows):
    return lax.dot_general(
        left, right_rows, (((1,), (1,)), ((), ())), preferred_element_type=F32
    )


def shifted(value, steps):
    count = lax.axis_size("x")
    first, last = max(0, -steps), min(count, count - steps)
    return lax.ppermute(value, "x", [(s, s + steps) for s in range(first, last)])


def swapped(value, axis):
    return lax.ppermute(value, axis, [(0, 1), (1, 0)])


def call(body, outs, scratch, flops, moved, scalar, *args, far=(), far_out=(), limit=VMEM_LIMIT):
    def spec(k, distant):
        return pl.BlockSpec(memory_space=pltpu.HBM if k in distant else pltpu.VMEM)

    specs = [spec(k, far) for k in range(len(args))]
    if scalar is not None:
        specs = [pl.BlockSpec(memory_space=pltpu.SMEM)] + specs
        args = (scalar,) + args
    return pl.pallas_call(
        body,
        out_shape=outs,
        in_specs=specs,
        out_specs=[spec(k, far_out) for k in range(len(outs))],
        scratch_shapes=scratch,
        compiler_params=pltpu.CompilerParams(vmem_limit_bytes=limit * 1024 * 1024),
        cost_estimate=pl.CostEstimate(flops=flops, bytes_accessed=moved, transcendentals=0),
    )(*args)


def pack_kernel(place, conv_far, proj_far, head_far, out, conv, proj, head, conv_wide, head_wide, sems):
    core, y, x = place[0], place[1], place[2]
    loads = [
        pltpu.make_async_copy(far, near, sems.at[k])
        for k, (far, near) in enumerate(((proj_far, proj), (conv_far, conv), (head_far, head)))
    ]
    for load in loads:
        load.start()
    granule, ch = out.shape[1], out.shape[2]
    tracks = head.shape[1]
    head_wide[:, tracks:] = jnp.zeros((head.shape[0], head_wide.shape[1] - tracks), F32)
    source = lax.broadcasted_iota(jnp.int32, (proj.shape[1], ch), 0)
    target = lax.broadcasted_iota(jnp.int32, (proj.shape[1], ch), 1)
    block = jnp.floor((target.astype(F32) + 0.5) * (1.0 / granule)).astype(jnp.int32)
    picked = (source == target + granule * block + granule * core).astype(F32).astype(BF)
    loads[0].wait()
    low = mm(proj[...], picked)
    loads[1].wait()
    conv_wide[...] = conv[...].astype(F32)
    loads[2].wait()
    head_wide[:, :tracks] = head[...].astype(F32)
    deep = conv.shape[0] // 2
    at = pl.multiple_of(core * deep + jnp.minimum(y, 2) * granule, 8)
    out[0] = jnp.where(y < 3, conv_wide[pl.ds(at, granule), :], low).astype(BF)
    out[1] = head_wide[
        pl.ds(pl.multiple_of(core * granule, 8), granule), pl.ds(pl.multiple_of(x * ch, 128), ch)
    ].astype(BF)


def copies_kernel(gathered, out):
    for k in range(out.shape[0]):
        out[k] = gathered[:, 0]


def prepare_kernel(
    core_ref, before, rows, following, gathered, early, taps_far, in_far, owner_far, head_far,
    tall, sorted_, kinds, owners, taps, ins, by_owner, sems
):
    stores = [
        pltpu.make_async_copy(gathered.at[:, 1], head_far.at[k], sems.at[k])
        for k in range(head_far.shape[0])
    ]
    for store in stores:
        store.start()
    core = core_ref[0]
    pos, width = rows.shape
    for at, source in enumerate((before, rows, following)):
        tall[at * width : (at + 1) * width, :] = jnp.transpose(source[...].astype(F32))
    count, granule = 16, 24
    deep = taps.shape[2]
    cut = 2 * deep // count
    for c in range(2):
        for y in range(3):
            for z in range(count):
                source = z * cut + c * (cut // 2) + y * granule
                target = (y * count + z) * granule
                sorted_[c, target : target + granule, :] = tall[source : source + granule, :]
        for z in range(count):
            source = width + (2 * z + c) * granule
            kinds[c, z * granule : (z + 1) * granule, :] = tall[source : source + granule, :]
    for k, at in enumerate((core, 1 - core)):
        taps[k] = jnp.transpose(sorted_[at]).astype(BF)
        ins[k] = jnp.transpose(kinds[at]).astype(BF)
    stores.append(pltpu.make_async_copy(taps, taps_far, sems.at[4]))
    stores.append(pltpu.make_async_copy(ins, in_far, sems.at[5]))
    for store in stores[4:]:
        store.start()
    owner_count = by_owner.shape[0]
    part = cut // owner_count
    for k in range(owner_count):
        for z in range(count):
            owners[k, z * part : (z + 1) * part, :] = tall[z * cut + k * part : z * cut + (k + 1) * part, :]
        by_owner[k] = owners[k].astype(BF)
    stores.append(pltpu.make_async_copy(by_owner, owner_far, sems.at[6]))
    stores[6].start()
    for store in stores:
        store.wait()


def conv_kernel(
    taps, ins, own, other, pre_ref, hid_own, hid_other
):
    ch = own.shape[1]
    deep = own.shape[0] - ch
    pre = mm(taps[0], own[:deep]) + mm(taps[1], other[:deep])
    pre_ref[...] = pre
    gated = gelu_tanh(pre).astype(BF)
    hid_own[...] = (ins[0].astype(F32) + mm(gated, own[deep:])).astype(BF)
    hid_other[...] = (ins[1].astype(F32) + mm(gated, other[deep:])).astype(BF)


def owned_kernel(yh_ref, source, out):
    yh = yh_ref[0]
    pos = source.shape[2]
    half = pos // 2
    pairs = source.shape[0] // 4
    left = lax.broadcasted_iota(jnp.int32, source.shape[1:], 1) < half
    for c in range(2):
        for k in range(pairs):
            even = source[4 * k + c].astype(F32)
            odd = source[4 * k + 2 + c].astype(F32)
            first = jnp.where(left, even, pltpu.roll(odd, half, 1))
            second = jnp.where(left, pltpu.roll(even, half, 1), odd)
            at = (c * pairs + k) * pos
            out[:, at : at + pos] = jnp.where(yh == 0, first, second).astype(BF)


def kernel_grad_kernel(owned, everyone, out, total, spaced):
    total[...] = mm(owned[...], everyone[...])
    spaced[...] = jnp.zeros_like(spaced)
    count = spaced.shape[0]
    part = total.shape[0] // count
    for z in range(count):
        spaced[z, :part, :] = total[z * part : (z + 1) * part, :]
    copies = out.shape[0] // count
    for z in range(count):
        for k in range(copies):
            out[z * copies + k] = spaced[z].astype(BF)


def input_grad_kernel(place, by_chip, hidden, own, other, out, grads, spread_, hid, total):
    core, x, yl = place[0], place[1], place[2]
    half, width = out.shape
    pos = 2 * half
    ch = own.shape[1]
    deep = own.shape[0] - ch
    last = by_chip.shape[0] // 2 - 1
    nil = jnp.zeros((half, ch), BF)
    following = by_chip[jnp.minimum(x + 1, last) * 2 + yl]
    before = by_chip[jnp.maximum(x - 1, 0) * 2 + yl]
    grads[:half] = jnp.where(x < last, following, nil)
    grads[half:pos] = nil
    grads[pos : pos + half] = by_chip[x * 2 + yl]
    grads[pos + half : 2 * pos] = nil
    grads[2 * pos : 2 * pos + half] = jnp.where(x > 0, before, nil)
    grads[2 * pos + half :] = nil
    spread_[core] = mm_t(own[:deep], grads[...])
    spread_[1 - core] = mm_t(other[:deep], grads[...])
    flipped = jnp.transpose(jnp.concatenate([hidden[...], jnp.zeros((half, width), F32)]))
    hid[core] = flipped[:ch]
    hid[1 - core] = flipped[ch:]
    granule, count = 24, 16
    for k in range(width // granule):
        block = hid[k % 2, (k // 2) * granule : (k // 2 + 1) * granule, :]
        for tap in range(3):
            row = tap * width + k * granule
            z, c, y = row // 144, (row % 144) // 72, (row % 72) // granule
            at = (y * count + z) * granule
            block = block + spread_[c, at : at + granule, tap * pos : (tap + 1) * pos]
        total[k * granule : (k + 1) * granule, :] = block
    out[...] = jnp.transpose(total[...])[:half]


def rows_of(first, second):
    pos = first.shape[0]
    lane = lax.broadcasted_iota(jnp.int32, (pos, pos), 1)
    return jnp.transpose(jnp.where(lane == 0, first, second))[:2]


def teacher_kernel(member, teacher, member_bias, assay, assay_temp, exp_ref, stats_ref):
    bias = member_bias[pl.ds(member[0], 1), :]
    temps = jnp.zeros(assay.shape, F32)
    for k in range(assay_temp.shape[1]):
        temps = jnp.where(assay[...] == k, assay_temp[:, k : k + 1], temps)
    target = (teacher[...].astype(F32) + bias) / temps
    peak = jnp.max(target, axis=1, keepdims=True)
    exps = jnp.exp(target - peak)
    exp_ref[...] = exps
    stats_ref[...] = rows_of(peak, jnp.sum(exps, axis=1, keepdims=True))


def columns_of(rows, count):
    return jnp.transpose(jnp.concatenate([rows, jnp.zeros((count - rows.shape[0], count), F32)]))


def head_kernel(hid_own, hid_other, own, other, target_stats, exp_ref, stats_ref):
    pos, tracks = exp_ref.shape
    wide = own.shape[2]
    for start in range(0, tracks, wide):
        n = min(wide, tracks - start)
        b = start // wide
        exp_ref[:, start : start + n] = mm(hid_own[...], own[b, :, :n]) + mm(
            hid_other[...], other[b, :, :n]
        )
    peak = jnp.max(exp_ref[...], axis=1, keepdims=True)
    exps = jnp.exp(exp_ref[...] - peak)
    exp_ref[...] = exps
    total = jnp.sum(exps, axis=1, keepdims=True)
    stats_ref[...] = jnp.concatenate([rows_of(peak, total), target_stats[...], jnp.zeros((4, pos), F32)])


def head_back_kernel(yh_ref, exp_s, exp_t, stats, own, other, kept_ref, sent_ref, hg):
    yh = yh_ref[0]
    pos, tracks = exp_s.shape
    wide, ch = own.shape[2], own.shape[1]
    half = pos // 2
    first, second = stats[0], stats[1]
    mine = jnp.where(yh == 0, first, second)

    def scale_of(at):
        top = jnp.maximum(first[at : at + 1], second[at : at + 1])
        total = first[at + 1 : at + 2] * jnp.exp(first[at : at + 1] - top) + second[
            at + 1 : at + 2
        ] * jnp.exp(second[at : at + 1] - top)
        return 2.0 * tracks * jnp.exp(mine[at : at + 1] - top) / total

    scales = columns_of(
        jnp.concatenate([scale_of(0), scale_of(2), jnp.zeros((6, pos), F32)]), pos
    )
    scale_s, scale_t = scales[:, 0:1], scales[:, 1:2]
    grad = (exp_s[...] * scale_s - exp_t[...] * scale_t).astype(BF)
    for source, at in ((own, 0), (other, ch)):
        total = None
        for start in range(0, tracks, wide):
            n = min(wide, tracks - start)
            term = mm_t(grad[:, start : start + n], source[start // wide, :, :n])
            total = term if total is None else total + term
        hg[:, at : at + ch] = total
    kept_ref[...] = hg[pl.ds(pl.multiple_of(yh * half, half), half), :]
    sent_ref[...] = hg[pl.ds(pl.multiple_of((1 - yh) * half, half), half), :].astype(BF)


def back_kernel(yh_ref, kept, received, pre_ref, own, other, grad_ref, hidden_ref):
    yh = yh_ref[0]
    half = kept.shape[0]
    ch = own.shape[1]
    hidden = kept[...] + received[...].astype(F32)
    hidden_ref[...] = hidden
    rounded = hidden.astype(BF)
    deep = own.shape[0] - ch
    gated_grad = mm_t(rounded[:, :ch], own[deep:]) + mm_t(rounded[:, ch:], other[deep:])
    pre = pre_ref[pl.ds(pl.multiple_of(yh * half, half), half), :]
    pre_grad = (gated_grad * gelu_slope(pre)).astype(BF)
    for k in range(grad_ref.shape[0]):
        grad_ref[k] = pre_grad


def on_device(
    inputs, teacher, member, member_bias, assay, assay_temp, conv_weight, proj_weight, head_weight
):
    rows = inputs[0]
    pos, width = rows.shape
    half = pos // 2
    cut, ch = conv_weight.shape
    tracks = head_weight.shape[1]
    zc, cc = lax.axis_size("z"), lax.axis_size(CTX)
    x, yl, core, yh = (lax.axis_index(name) for name in ("x", "yl", "c", "yh"))
    yh_arr = yh.astype(jnp.int32).reshape(1)

    slab = 24
    deep = cut // 2
    deep = cut // 2
    place = jnp.stack([core, yl * 2 + yh, x]).astype(jnp.int32)
    (packed,) = call(
        pack_kernel,
        [SDS((2, slab, ch), BF)],
        [
            pltpu.VMEM(conv_weight.shape, BF),
            pltpu.VMEM(proj_weight.shape, BF),
            pltpu.VMEM(head_weight.shape, BF),
            pltpu.VMEM((cut, ch), F32),
            pltpu.VMEM((2 * slab, 4 * ch), F32),
            pltpu.SemaphoreType.DMA((3,)),
        ],
        2 * slab * width * ch,
        512 * 1024,
        place,
        conv_weight,
        proj_weight,
        head_weight,
        far=(0, 1, 2),
        limit=56,
    )
    gathered = lax.all_gather(packed, "z", axis=0)
    (conv_copies,) = call(
        copies_kernel, [SDS((4, zc, slab, ch), BF)], [], 1024, 1536 * 1024, None, gathered
    )
    over_y = lax.all_to_all(conv_copies, YR, 0, 0).reshape(4 * zc * slab, ch)
    rows_before = shifted(rows, 1)
    rows_after = shifted(rows, -1)
    exp_t, target_stats = call(
        teacher_kernel,
        [SDS((pos, tracks), F32), SDS((2, pos), F32)],
        [],
        4 * pos * tracks,
        1536 * 1024,
        member.astype(jnp.int32),
        teacher[0],
        member_bias,
        assay.reshape(1, tracks),
        assay_temp.reshape(1, assay_temp.shape[0]),
        limit=56,
    )
    own = over_y
    other = swapped(own, "c")

    part = cut // cc
    core_arr = core.astype(jnp.int32).reshape(1)
    taps, kinds, by_owner, head_copies = call(
        prepare_kernel,
        [
            SDS((2, pos, zc * deep), BF),
            SDS((2, pos, ch), BF),
            SDS((cc, zc * part, pos), BF),
            SDS((4, zc, slab, ch), BF),
        ],
        [
            pltpu.VMEM((3 * width, pos), F32),
            pltpu.VMEM((2, zc * deep, pos), F32),
            pltpu.VMEM((2, ch, pos), F32),
            pltpu.VMEM((cc, zc * part, pos), F32),
            pltpu.VMEM((2, pos, zc * deep), BF),
            pltpu.VMEM((2, pos, ch), BF),
            pltpu.VMEM((cc, zc * part, pos), BF),
            pltpu.SemaphoreType.DMA((7,)),
        ],
        2 * pos * pos * 3 * width,
        2 * 1024 * 1024,
        core_arr,
        rows_before,
        rows,
        rows_after,
        gathered,
        target_stats,
        far_out=(0, 1, 2, 3),
        limit=56,
    )
    head_own = lax.all_to_all(head_copies, "x", 0, 0).reshape(4, zc * slab, ch)
    pre_act, hid_own, hid_other = call(
        conv_kernel,
        [SDS((pos, ch), F32), SDS((pos, ch), BF), SDS((pos, ch), BF)],
        [],
        2 * pos * ch * 4 * width,
        3 * 1024 * 1024,
        None,
        taps,
        kinds,
        own,
        other,
    )

    head_other = swapped(head_own, "c")

    owned = lax.all_to_all(by_owner, CTX, 0, 0)
    (owned,) = call(
        owned_kernel,
        [SDS((zc * part, cc * half), BF)],
        [],
        1024 * 1024,
        1024 * 1024,
        yh_arr,
        owned,
    )

    exp_s, stats = call(
        head_kernel,
        [SDS((pos, tracks), F32), SDS((8, pos), F32)],
        [],
        2 * pos * width * tracks,
        4 * 1024 * 1024,
        None,
        hid_own,
        hid_other,
        head_own,
        head_other,
        target_stats,
    )
    stats = lax.all_gather(stats, "yh", axis=0)
    kept, sent = call(
        head_back_kernel,
        [SDS((half, width), F32), SDS((half, width), BF)],
        [pltpu.VMEM((pos, width), F32)],
        2 * pos * width * tracks,
        4 * 1024 * 1024,
        yh_arr,
        exp_s,
        exp_t,
        stats,
        head_own,
        head_other,
    )
    received = swapped(sent, "yh")
    copies, hidden_grad = call(
        back_kernel,
        [SDS((cc // 2, half, ch), BF), SDS((half, width), F32)],
        [],
        2 * half * width * ch,
        2 * 1024 * 1024,
        yh_arr,
        kept,
        received,
        pre_act,
        own,
        other,
    )

    by_chip = lax.all_to_all(copies, ("x", "yl"), 0, 0)
    everyone = lax.all_gather(by_chip.reshape(cc // 2 * half, ch), "c", axis=0, tiled=True)
    padded = 16
    (kernel_part,) = call(
        kernel_grad_kernel,
        [SDS((zc, padded, ch), BF)],
        [pltpu.VMEM((zc * part, ch), F32), pltpu.VMEM((zc, padded, ch), F32)],
        2 * zc * part * cc * half * ch,
        2 * 1024 * 1024,
        None,
        owned,
        everyone,
    )
    terms = lax.all_to_all(kernel_part, "z", 0, 0)
    kernel_sum = jnp.sum(terms.astype(F32), axis=0)[:part]
    kernel_pair = lax.all_gather(kernel_sum, "yh", axis=0)
    grad_conv = (kernel_pair[0] + kernel_pair[1]) / math.sqrt(zc * cc * pos)

    (grad_rows,) = call(
        input_grad_kernel,
        [SDS((half, width), F32)],
        [
            pltpu.VMEM((3 * pos, ch), BF),
            pltpu.VMEM((2, zc * deep, 3 * pos), F32),
            pltpu.VMEM((2, ch, pos), F32),
            pltpu.VMEM((width, pos), F32),
        ],
        4 * half * width * ch,
        2 * 1024 * 1024,
        jnp.stack([core, x, yl]).astype(jnp.int32),
        by_chip,
        hidden_grad,
        own,
        other,
    )
    grad_other = swapped(grad_rows, "yh")
    grad_input = jnp.where(
        yh == 0,
        jnp.concatenate([grad_rows, grad_other], axis=0),
        jnp.concatenate([grad_other, grad_rows], axis=0),
    )
    return (grad_input[None], grad_conv)


def solution(mesh):
    fine = Mesh(mesh.devices.reshape(16, 4, 2, 2, 2), ("z", "x", "yl", "c", "yh"))
    return jax.shard_map(
        on_device,
        mesh=fine,
        in_specs=(
            P("z", CTX, None),
            P("z", CTX, "yh"),
            P("z"),
            P(None, "yh"),
            P("yh"),
            P(),
            P("z", None),
            P("z", None),
            P("z", "yh"),
        ),
        out_specs=(P("z", CTX, None), P(("z",) + CTX, None)),
        check_vma=False,
    )
```

```python
import functools
import math

import jax
import jax.numpy as jnp
from jax import lax
from jax.experimental import pallas as pl
from jax.experimental.pallas import tpu as pltpu
from jax.sharding import Mesh, PartitionSpec as P

BF = jnp.bfloat16
F32 = jnp.float32
CTX = ("x", "yl", "c")
YR = ("yl", "yh")
VMEM_LIMIT = 12
CURVE = 0.044715
SLOPE = math.sqrt(2.0 / math.pi)
SDS = jax.ShapeDtypeStruct


def gelu_tanh(values):
    return 0.5 * values * (1.0 + jnp.tanh(SLOPE * (values + CURVE * values * values * values)))


def gelu_slope(values):
    square = values * values
    bend = jnp.tanh(SLOPE * (values + CURVE * values * square))
    return 0.5 * (1.0 + bend) + 0.5 * values * (1.0 - bend * bend) * SLOPE * (
        1.0 + 3.0 * CURVE * square
    )


def mm(left, right):
    return jnp.dot(left, right, preferred_element_type=F32)


def mm_t(left, right_rows):
    return lax.dot_general(
        left, right_rows, (((1,), (1,)), ((), ())), preferred_element_type=F32
    )


def shifted(value, steps):
    count = lax.axis_size("x")
    first, last = max(0, -steps), min(count, count - steps)
    return lax.ppermute(value, "x", [(s, s + steps) for s in range(first, last)])


def swapped(value, axis):
    return lax.ppermute(value, axis, [(0, 1), (1, 0)])


def call(body, outs, scratch, flops, moved, scalar, *args, far=(), far_out=(), limit=VMEM_LIMIT):
    def spec(k, distant):
        return pl.BlockSpec(memory_space=pltpu.HBM if k in distant else pltpu.VMEM)

    specs = [spec(k, far) for k in range(len(args))]
    if scalar is not None:
        specs = [pl.BlockSpec(memory_space=pltpu.SMEM)] + specs
        args = (scalar,) + args
    return pl.pallas_call(
        body,
        out_shape=outs,
        in_specs=specs,
        out_specs=[spec(k, far_out) for k in range(len(outs))],
        scratch_shapes=scratch,
        compiler_params=pltpu.CompilerParams(vmem_limit_bytes=limit * 1024 * 1024),
        cost_estimate=pl.CostEstimate(flops=flops, bytes_accessed=moved, transcendentals=0),
    )(*args)


def pack_kernel(conv_far, proj_far, head_far, out, conv, proj, head, conv_wide, head_wide, sems):
    core, x = lax.axis_index("c"), lax.axis_index("x")
    y = lax.axis_index("yl") * 2 + lax.axis_index("yh")
    loads = [
        pltpu.make_async_copy(far, near, sems.at[k])
        for k, (far, near) in enumerate(((proj_far, proj), (conv_far, conv), (head_far, head)))
    ]
    for load in loads:
        load.start()
    granule, ch = out.shape[1], out.shape[2]
    tracks = head.shape[1]
    head_wide[:, tracks:] = jnp.zeros((head.shape[0], head_wide.shape[1] - tracks), F32)
    source = lax.broadcasted_iota(jnp.int32, (proj.shape[1], ch), 0)
    target = lax.broadcasted_iota(jnp.int32, (proj.shape[1], ch), 1)
    block = jnp.floor((target.astype(F32) + 0.5) * (1.0 / granule)).astype(jnp.int32)
    picked = (source == target + granule * block + granule * core).astype(F32).astype(BF)
    loads[0].wait()
    low = mm(proj[...], picked)
    loads[1].wait()
    conv_wide[...] = conv[...].astype(F32)
    loads[2].wait()
    head_wide[:, :tracks] = head[...].astype(F32)
    deep = conv.shape[0] // 2
    at = pl.multiple_of(core * deep + jnp.minimum(y, 2) * granule, 8)
    out[0] = jnp.where(y < 3, conv_wide[pl.ds(at, granule), :], low).astype(BF)
    out[1] = head_wide[
        pl.ds(pl.multiple_of(core * granule, 8), granule), pl.ds(pl.multiple_of(x * ch, 128), ch)
    ].astype(BF)


def copies_kernel(gathered, out):
    for k in range(out.shape[0]):
        out[k] = gathered[:, 0]


def prepare_kernel(
    core_ref, before, rows, following, gathered, early, taps_far, in_far, owner_far, head_far,
    tall, sorted_, kinds, owners, taps, ins, by_owner, sems
):
    stores = [
        pltpu.make_async_copy(gathered.at[:, 1], head_far.at[k], sems.at[k])
        for k in range(head_far.shape[0])
    ]
    for store in stores:
        store.start()
    core = core_ref[0]
    pos, width = rows.shape
    for at, source in enumerate((before, rows, following)):
        tall[at * width : (at + 1) * width, :] = jnp.transpose(source[...].astype(F32))
    count, granule = 16, 24
    deep = taps.shape[2]
    cut = 2 * deep // count
    for c in range(2):
        for y in range(3):
            for z in range(count):
                source = z * cut + c * (cut // 2) + y * granule
                target = (y * count + z) * granule
                sorted_[c, target : target + granule, :] = tall[source : source + granule, :]
        for z in range(count):
            source = width + (2 * z + c) * granule
            kinds[c, z * granule : (z + 1) * granule, :] = tall[source : source + granule, :]
    for k, at in enumerate((core, 1 - core)):
        taps[k] = jnp.transpose(sorted_[at]).astype(BF)
        ins[k] = jnp.transpose(kinds[at]).astype(BF)
    stores.append(pltpu.make_async_copy(taps, taps_far, sems.at[4]))
    stores.append(pltpu.make_async_copy(ins, in_far, sems.at[5]))
    for store in stores[4:]:
        store.start()
    owner_count = by_owner.shape[0]
    part = cut // owner_count
    for k in range(owner_count):
        for z in range(count):
            owners[k, z * part : (z + 1) * part, :] = tall[z * cut + k * part : z * cut + (k + 1) * part, :]
        by_owner[k] = owners[k].astype(BF)
    stores.append(pltpu.make_async_copy(by_owner, owner_far, sems.at[6]))
    stores[6].start()
    for store in stores:
        store.wait()


def conv_kernel(taps, own, other, pre_ref, gated_ref):
    deep = taps.shape[2]
    pre = mm(taps[0], own[:deep]) + mm(taps[1], other[:deep])
    pre_ref[...] = pre
    gated_ref[...] = gelu_tanh(pre).astype(BF)


def hidden_kernel(gated, ins, own, other, hid_own, hid_other):
    deep = own.shape[0] - own.shape[1]
    hid_own[...] = (ins[0].astype(F32) + mm(gated[...], own[deep:])).astype(BF)
    hid_other[...] = (ins[1].astype(F32) + mm(gated[...], other[deep:])).astype(BF)


def owned_kernel(yh_ref, source, out):
    yh = yh_ref[0]
    pos = source.shape[2]
    half = pos // 2
    pairs = source.shape[0] // 4
    left = lax.broadcasted_iota(jnp.int32, source.shape[1:], 1) < half
    for c in range(2):
        for k in range(pairs):
            even = source[4 * k + c].astype(F32)
            odd = source[4 * k + 2 + c].astype(F32)
            first = jnp.where(left, even, pltpu.roll(odd, half, 1))
            second = jnp.where(left, pltpu.roll(even, half, 1), odd)
            at = (c * pairs + k) * pos
            out[:, at : at + pos] = jnp.where(yh == 0, first, second).astype(BF)


def kernel_grad_kernel(owned, everyone, out, total, spaced):
    total[...] = mm(owned[...], everyone[...])
    spaced[...] = jnp.zeros_like(spaced)
    count = spaced.shape[0]
    part = total.shape[0] // count
    for z in range(count):
        spaced[z, :part, :] = total[z * part : (z + 1) * part, :]
    copies = out.shape[0] // count
    for z in range(count):
        for k in range(copies):
            out[z * copies + k] = spaced[z].astype(BF)


def input_grad_kernel(place, by_chip, hidden, own, other, out, grads, spread_, hid, total):
    core, x, yl = place[0], place[1], place[2]
    half, width = out.shape
    pos = 2 * half
    ch = own.shape[1]
    deep = own.shape[0] - ch
    last = by_chip.shape[0] // 2 - 1
    nil = jnp.zeros((half, ch), BF)
    following = by_chip[jnp.minimum(x + 1, last) * 2 + yl]
    before = by_chip[jnp.maximum(x - 1, 0) * 2 + yl]
    grads[:half] = jnp.where(x < last, following, nil)
    grads[half:pos] = nil
    grads[pos : pos + half] = by_chip[x * 2 + yl]
    grads[pos + half : 2 * pos] = nil
    grads[2 * pos : 2 * pos + half] = jnp.where(x > 0, before, nil)
    grads[2 * pos + half :] = nil
    spread_[core] = mm_t(own[:deep], grads[...])
    spread_[1 - core] = mm_t(other[:deep], grads[...])
    flipped = jnp.transpose(jnp.concatenate([hidden[...], jnp.zeros((half, width), F32)]))
    hid[core] = flipped[:ch]
    hid[1 - core] = flipped[ch:]
    granule, count = 24, 16
    for k in range(width // granule):
        block = hid[k % 2, (k // 2) * granule : (k // 2 + 1) * granule, :]
        for tap in range(3):
            row = tap * width + k * granule
            z, c, y = row // 144, (row % 144) // 72, (row % 72) // granule
            at = (y * count + z) * granule
            block = block + spread_[c, at : at + granule, tap * pos : (tap + 1) * pos]
        total[k * granule : (k + 1) * granule, :] = block
    out[...] = jnp.transpose(total[...])[:half]


def rows_of(first, second):
    pos = first.shape[0]
    lane = lax.broadcasted_iota(jnp.int32, (pos, pos), 1)
    return jnp.transpose(jnp.where(lane == 0, first, second))[:2]


def teacher_kernel(member, teacher, member_bias, assay, assay_temp, exp_ref, stats_ref):
    bias = member_bias[pl.ds(member[0], 1), :]
    groups = assay[...][None, :]
    temps = jnp.zeros(groups.shape, F32)
    for k in range(assay_temp.shape[1]):
        temps = jnp.where(groups == k, assay_temp[:, k : k + 1], temps)
    target = (teacher[...].astype(F32) + bias) / temps
    peak = jnp.max(target, axis=1, keepdims=True)
    exps = jnp.exp(target - peak)
    exp_ref[...] = exps
    stats_ref[...] = rows_of(peak, jnp.sum(exps, axis=1, keepdims=True))


def columns_of(rows, count):
    return jnp.transpose(jnp.concatenate([rows, jnp.zeros((count - rows.shape[0], count), F32)]))


def head_kernel(hid_own, hid_other, own, other, target_stats, exp_ref, stats_ref):
    pos, tracks = exp_ref.shape
    wide = own.shape[2]
    for start in range(0, tracks, wide):
        n = min(wide, tracks - start)
        b = start // wide
        exp_ref[:, start : start + n] = mm(hid_own[...], own[b, :, :n]) + mm(
            hid_other[...], other[b, :, :n]
        )
    peak = jnp.max(exp_ref[...], axis=1, keepdims=True)
    exps = jnp.exp(exp_ref[...] - peak)
    exp_ref[...] = exps
    total = jnp.sum(exps, axis=1, keepdims=True)
    stats_ref[...] = jnp.concatenate([rows_of(peak, total), target_stats[...], jnp.zeros((4, pos), F32)])


def head_back_kernel(yh_ref, exp_s, exp_t, stats, own, other, kept_ref, sent_ref, hg):
    yh = yh_ref[0]
    pos, tracks = exp_s.shape
    wide, ch = own.shape[2], own.shape[1]
    half = pos // 2
    first, second = stats[0], stats[1]
    mine = jnp.where(yh == 0, first, second)

    def scale_of(at):
        top = jnp.maximum(first[at : at + 1], second[at : at + 1])
        total = first[at + 1 : at + 2] * jnp.exp(first[at : at + 1] - top) + second[
            at + 1 : at + 2
        ] * jnp.exp(second[at : at + 1] - top)
        return 2.0 * tracks * jnp.exp(mine[at : at + 1] - top) / total

    scales = columns_of(
        jnp.concatenate([scale_of(0), scale_of(2), jnp.zeros((6, pos), F32)]), pos
    )
    scale_s, scale_t = scales[:, 0:1], scales[:, 1:2]
    grad = (exp_s[...] * scale_s - exp_t[...] * scale_t).astype(BF)
    for source, at in ((own, 0), (other, ch)):
        total = None
        for start in range(0, tracks, wide):
            n = min(wide, tracks - start)
            term = mm_t(grad[:, start : start + n], source[start // wide, :, :n])
            total = term if total is None else total + term
        hg[:, at : at + ch] = total
    kept_ref[...] = hg[pl.ds(pl.multiple_of(yh * half, half), half), :]
    sent_ref[...] = hg[pl.ds(pl.multiple_of((1 - yh) * half, half), half), :].astype(BF)


def back_kernel(yh_ref, kept, received, pre_ref, own, other, grad_ref, hidden_ref):
    yh = yh_ref[0]
    half = kept.shape[0]
    ch = own.shape[1]
    hidden = kept[...] + received[...].astype(F32)
    hidden_ref[...] = hidden
    rounded = hidden.astype(BF)
    deep = own.shape[0] - ch
    gated_grad = mm_t(rounded[:, :ch], own[deep:]) + mm_t(rounded[:, ch:], other[deep:])
    pre = pre_ref[pl.ds(pl.multiple_of(yh * half, half), half), :]
    pre_grad = (gated_grad * gelu_slope(pre)).astype(BF)
    for k in range(grad_ref.shape[0]):
        grad_ref[k] = pre_grad


def on_device(
    inputs, teacher, member, member_bias, assay, assay_temp, conv_weight, proj_weight, head_weight
):
    rows = inputs[0]
    pos, width = rows.shape
    half = pos // 2
    cut, ch = conv_weight.shape
    tracks = head_weight.shape[1]
    zc, cc = lax.axis_size("z"), lax.axis_size(CTX)
    x, yl, core, yh = (lax.axis_index(name) for name in ("x", "yl", "c", "yh"))
    yh_arr = yh.astype(jnp.int32).reshape(1)

    slab = 24
    deep = cut // 2
    deep = cut // 2
    (packed,) = call(
        pack_kernel,
        [SDS((2, slab, ch), BF)],
        [
            pltpu.VMEM(conv_weight.shape, BF),
            pltpu.VMEM(proj_weight.shape, BF),
            pltpu.VMEM(head_weight.shape, BF),
            pltpu.VMEM((cut, ch), F32),
            pltpu.VMEM((2 * slab, 4 * ch), F32),
            pltpu.SemaphoreType.DMA((3,)),
        ],
        2 * slab * width * ch,
        512 * 1024,
        None,
        conv_weight,
        proj_weight,
        head_weight,
        far=(0, 1, 2),
        limit=56,
    )
    gathered = lax.all_gather(packed, "z", axis=0)
    (conv_copies,) = call(
        copies_kernel, [SDS((4, zc, slab, ch), BF)], [], 1024, 1536 * 1024, None, gathered
    )
    over_y = lax.all_to_all(conv_copies, YR, 0, 0).reshape(4 * zc * slab, ch)
    rows_before = shifted(rows, 1)
    rows_after = shifted(rows, -1)
    exp_t, target_stats = call(
        teacher_kernel,
        [SDS((pos, tracks), F32), SDS((2, pos), F32)],
        [],
        4 * pos * tracks,
        1536 * 1024,
        member.astype(jnp.int32),
        teacher[0],
        member_bias,
        assay,
        assay_temp.reshape(1, assay_temp.shape[0]),
        limit=56,
    )
    own = over_y
    other = swapped(own, "c")

    part = cut // cc
    core_arr = core.astype(jnp.int32).reshape(1)
    taps, kinds, by_owner, head_copies = call(
        prepare_kernel,
        [
            SDS((2, pos, zc * deep), BF),
            SDS((2, pos, ch), BF),
            SDS((cc, zc * part, pos), BF),
            SDS((4, zc, slab, ch), BF),
        ],
        [
            pltpu.VMEM((3 * width, pos), F32),
            pltpu.VMEM((2, zc * deep, pos), F32),
            pltpu.VMEM((2, ch, pos), F32),
            pltpu.VMEM((cc, zc * part, pos), F32),
            pltpu.VMEM((2, pos, zc * deep), BF),
            pltpu.VMEM((2, pos, ch), BF),
            pltpu.VMEM((cc, zc * part, pos), BF),
            pltpu.SemaphoreType.DMA((7,)),
        ],
        2 * pos * pos * 3 * width,
        2 * 1024 * 1024,
        core_arr,
        rows_before,
        rows,
        rows_after,
        gathered,
        target_stats,
        far_out=(0, 1, 2, 3),
        limit=56,
    )
    head_own = lax.all_to_all(head_copies, "x", 0, 0).reshape(4, zc * slab, ch)
    pre_act, gated = call(
        conv_kernel,
        [SDS((pos, ch), F32), SDS((pos, ch), BF)],
        [],
        2 * pos * ch * 3 * width,
        3 * 1024 * 1024,
        None,
        taps,
        own,
        other,
    )
    hid_own, hid_other = call(
        hidden_kernel,
        [SDS((pos, ch), BF), SDS((pos, ch), BF)],
        [],
        2 * pos * ch * width,
        1024 * 1024,
        None,
        gated,
        kinds,
        own,
        other,
    )
    head_other = swapped(head_own, "c")

    owned = lax.all_to_all(by_owner, CTX, 0, 0)
    (owned,) = call(
        owned_kernel,
        [SDS((zc * part, cc * half), BF)],
        [],
        1024 * 1024,
        1024 * 1024,
        yh_arr,
        owned,
    )

    exp_s, stats = call(
        head_kernel,
        [SDS((pos, tracks), F32), SDS((8, pos), F32)],
        [],
        2 * pos * width * tracks,
        4 * 1024 * 1024,
        None,
        hid_own,
        hid_other,
        head_own,
        head_other,
        target_stats,
    )
    stats = lax.all_gather(stats, "yh", axis=0)
    kept, sent = call(
        head_back_kernel,
        [SDS((half, width), F32), SDS((half, width), BF)],
        [pltpu.VMEM((pos, width), F32)],
        2 * pos * width * tracks,
        4 * 1024 * 1024,
        yh_arr,
        exp_s,
        exp_t,
        stats,
        head_own,
        head_other,
    )
    received = swapped(sent, "yh")
    copies, hidden_grad = call(
        back_kernel,
        [SDS((cc // 2, half, ch), BF), SDS((half, width), F32)],
        [],
        2 * half * width * ch,
        2 * 1024 * 1024,
        yh_arr,
        kept,
        received,
        pre_act,
        own,
        other,
    )

    by_chip = lax.all_to_all(copies, ("x", "yl"), 0, 0)
    everyone = lax.all_gather(by_chip.reshape(cc // 2 * half, ch), "c", axis=0, tiled=True)
    padded = 16
    (kernel_part,) = call(
        kernel_grad_kernel,
        [SDS((zc, padded, ch), BF)],
        [pltpu.VMEM((zc * part, ch), F32), pltpu.VMEM((zc, padded, ch), F32)],
        2 * zc * part * cc * half * ch,
        2 * 1024 * 1024,
        None,
        owned,
        everyone,
    )
    terms = lax.all_to_all(kernel_part, "z", 0, 0)
    kernel_sum = jnp.sum(terms.astype(F32), axis=0)[:part]
    kernel_pair = lax.all_gather(kernel_sum, "yh", axis=0)
    grad_conv = (kernel_pair[0] + kernel_pair[1]) / math.sqrt(zc * cc * pos)

    (grad_rows,) = call(
        input_grad_kernel,
        [SDS((half, width), F32)],
        [
            pltpu.VMEM((3 * pos, ch), BF),
            pltpu.VMEM((2, zc * deep, 3 * pos), F32),
            pltpu.VMEM((2, ch, pos), F32),
            pltpu.VMEM((width, pos), F32),
        ],
        4 * half * width * ch,
        2 * 1024 * 1024,
        jnp.stack([core, x, yl]).astype(jnp.int32),
        by_chip,
        hidden_grad,
        own,
        other,
    )
    grad_other = swapped(grad_rows, "yh")
    grad_input = jnp.where(
        yh == 0,
        jnp.concatenate([grad_rows, grad_other], axis=0),
        jnp.concatenate([grad_other, grad_rows], axis=0),
    )
    return (grad_input[None], grad_conv)


def solution(mesh):
    fine = Mesh(mesh.devices.reshape(16, 4, 2, 2, 2), ("z", "x", "yl", "c", "yh"))
    return jax.shard_map(
        on_device,
        mesh=fine,
        in_specs=(
            P("z", CTX, None),
            P("z", CTX, "yh"),
            P("z"),
            P(None, "yh"),
            P("yh"),
            P(),
            P("z", None),
            P("z", None),
            P("z", "yh"),
        ),
        out_specs=(P("z", CTX, None), P(("z",) + CTX, None)),
        check_vma=False,
    )
```

```python
import functools
import math

import jax
import jax.numpy as jnp
from jax import lax
from jax.experimental import pallas as pl
from jax.experimental.pallas import tpu as pltpu
from jax.sharding import Mesh, PartitionSpec as P

BF = jnp.bfloat16
F32 = jnp.float32
CTX = ("x", "yl", "c")
YR = ("yl", "yh")
VMEM_LIMIT = 12
CURVE = 0.044715
SLOPE = math.sqrt(2.0 / math.pi)
SDS = jax.ShapeDtypeStruct


def gelu_tanh(values):
    return 0.5 * values * (1.0 + jnp.tanh(SLOPE * (values + CURVE * values * values * values)))


def gelu_slope(values):
    square = values * values
    bend = jnp.tanh(SLOPE * (values + CURVE * values * square))
    return 0.5 * (1.0 + bend) + 0.5 * values * (1.0 - bend * bend) * SLOPE * (
        1.0 + 3.0 * CURVE * square
    )


def mm(left, right):
    return jnp.dot(left, right, preferred_element_type=F32)


def mm_t(left, right_rows):
    return lax.dot_general(
        left, right_rows, (((1,), (1,)), ((), ())), preferred_element_type=F32
    )


def shifted(value, steps):
    count = lax.axis_size("x")
    first, last = max(0, -steps), min(count, count - steps)
    return lax.ppermute(value, "x", [(s, s + steps) for s in range(first, last)])


def swapped(value, axis):
    return lax.ppermute(value, axis, [(0, 1), (1, 0)])


def call(body, outs, scratch, flops, moved, scalar, *args, far=(), far_out=(), limit=VMEM_LIMIT):
    def spec(k, distant):
        return pl.BlockSpec(memory_space=pltpu.HBM if k in distant else pltpu.VMEM)

    specs = [spec(k, far) for k in range(len(args))]
    if scalar is not None:
        specs = [pl.BlockSpec(memory_space=pltpu.SMEM)] + specs
        args = (scalar,) + args
    return pl.pallas_call(
        body,
        out_shape=outs,
        in_specs=specs,
        out_specs=[spec(k, far_out) for k in range(len(outs))],
        scratch_shapes=scratch,
        compiler_params=pltpu.CompilerParams(vmem_limit_bytes=limit * 1024 * 1024),
        cost_estimate=pl.CostEstimate(flops=flops, bytes_accessed=moved, transcendentals=0),
    )(*args)


def pack_kernel(conv_far, proj_far, head_far, out, conv, proj, head, conv_wide, head_wide, sems):
    core, x = lax.axis_index("c"), lax.axis_index("x")
    y = lax.axis_index("yl") * 2 + lax.axis_index("yh")
    loads = [
        pltpu.make_async_copy(far, near, sems.at[k])
        for k, (far, near) in enumerate(((proj_far, proj), (conv_far, conv), (head_far, head)))
    ]
    for load in loads:
        load.start()
    granule, ch = out.shape[1], out.shape[2]
    tracks = head.shape[1]
    head_wide[:, tracks:] = jnp.zeros((head.shape[0], head_wide.shape[1] - tracks), F32)
    source = lax.broadcasted_iota(jnp.int32, (proj.shape[1], ch), 0)
    target = lax.broadcasted_iota(jnp.int32, (proj.shape[1], ch), 1)
    block = jnp.floor((target.astype(F32) + 0.5) * (1.0 / granule)).astype(jnp.int32)
    picked = (source == target + granule * block + granule * core).astype(F32).astype(BF)
    loads[0].wait()
    low = mm(proj[...], picked)
    loads[1].wait()
    conv_wide[...] = conv[...].astype(F32)
    loads[2].wait()
    head_wide[:, :tracks] = head[...].astype(F32)
    deep = conv.shape[0] // 2
    at = pl.multiple_of(core * deep + jnp.minimum(y, 2) * granule, 8)
    out[0] = jnp.where(y < 3, conv_wide[pl.ds(at, granule), :], low).astype(BF)
    out[1] = head_wide[
        pl.ds(pl.multiple_of(core * granule, 8), granule), pl.ds(pl.multiple_of(x * ch, 128), ch)
    ].astype(BF)


def copies_kernel(gathered, out):
    for k in range(out.shape[0]):
        out[k] = gathered[:, 0]


def prepare_kernel(
    core_ref, before, rows, following, gathered, early, taps_far, in_far, owner_far, head_far,
    tall, sorted_, kinds, owners, taps, ins, by_owner, sems
):
    stores = [
        pltpu.make_async_copy(gathered.at[:, 1], head_far.at[k], sems.at[k])
        for k in range(head_far.shape[0])
    ]
    for store in stores:
        store.start()
    core = core_ref[0]
    pos, width = rows.shape
    for at, source in enumerate((before, rows, following)):
        tall[at * width : (at + 1) * width, :] = jnp.transpose(source[...].astype(F32))
    count, granule = 16, 24
    deep = taps.shape[2]
    cut = 2 * deep // count
    for c in range(2):
        for y in range(3):
            for z in range(count):
                source = z * cut + c * (cut // 2) + y * granule
                target = (y * count + z) * granule
                sorted_[c, target : target + granule, :] = tall[source : source + granule, :]
        for z in range(count):
            source = width + (2 * z + c) * granule
            kinds[c, z * granule : (z + 1) * granule, :] = tall[source : source + granule, :]
    for k, at in enumerate((core, 1 - core)):
        taps[k] = jnp.transpose(sorted_[at]).astype(BF)
        ins[k] = jnp.transpose(kinds[at]).astype(BF)
    stores.append(pltpu.make_async_copy(taps, taps_far, sems.at[4]))
    stores.append(pltpu.make_async_copy(ins, in_far, sems.at[5]))
    for store in stores[4:]:
        store.start()
    owner_count = by_owner.shape[0]
    part = cut // owner_count
    for k in range(owner_count):
        for z in range(count):
            owners[k, z * part : (z + 1) * part, :] = tall[z * cut + k * part : z * cut + (k + 1) * part, :]
        by_owner[k] = owners[k].astype(BF)
    stores.append(pltpu.make_async_copy(by_owner, owner_far, sems.at[6]))
    stores[6].start()
    for store in stores:
        store.wait()


def conv_kernel(taps, own, other, pre_ref, gated_ref):
    deep = taps.shape[2]
    pre = mm(taps[0], own[:deep]) + mm(taps[1], other[:deep])
    pre_ref[...] = pre
    gated_ref[...] = gelu_tanh(pre).astype(BF)


def hidden_kernel(gated, ins, own, other, hid_own, hid_other):
    deep = own.shape[0] - own.shape[1]
    hid_own[...] = (ins[0].astype(F32) + mm(gated[...], own[deep:])).astype(BF)
    hid_other[...] = (ins[1].astype(F32) + mm(gated[...], other[deep:])).astype(BF)


def owned_kernel(yh_ref, source, out):
    yh = yh_ref[0]
    pos = source.shape[2]
    half = pos // 2
    pairs = source.shape[0] // 4
    left = lax.broadcasted_iota(jnp.int32, source.shape[1:], 1) < half
    for c in range(2):
        for k in range(pairs):
            even = source[4 * k + c].astype(F32)
            odd = source[4 * k + 2 + c].astype(F32)
            first = jnp.where(left, even, pltpu.roll(odd, half, 1))
            second = jnp.where(left, pltpu.roll(even, half, 1), odd)
            at = (c * pairs + k) * pos
            out[:, at : at + pos] = jnp.where(yh == 0, first, second).astype(BF)


def kernel_grad_kernel(owned, everyone, out, total, spaced):
    total[...] = mm(owned[...], everyone[...])
    spaced[...] = jnp.zeros_like(spaced)
    count = spaced.shape[0]
    part = total.shape[0] // count
    for z in range(count):
        spaced[z, :part, :] = total[z * part : (z + 1) * part, :]
    copies = out.shape[0] // count
    for z in range(count):
        for k in range(copies):
            out[z * copies + k] = spaced[z].astype(BF)


def input_grad_kernel(place, by_chip, hidden, own, other, out, grads, spread_, hid, total):
    core, x, yl = place[0], place[1], place[2]
    half, width = out.shape
    pos = 2 * half
    ch = own.shape[1]
    deep = own.shape[0] - ch
    last = by_chip.shape[0] // 2 - 1
    nil = jnp.zeros((half, ch), BF)
    following = by_chip[jnp.minimum(x + 1, last) * 2 + yl]
    before = by_chip[jnp.maximum(x - 1, 0) * 2 + yl]
    grads[:half] = jnp.where(x < last, following, nil)
    grads[half:pos] = nil
    grads[pos : pos + half] = by_chip[x * 2 + yl]
    grads[pos + half : 2 * pos] = nil
    grads[2 * pos : 2 * pos + half] = jnp.where(x > 0, before, nil)
    grads[2 * pos + half :] = nil
    spread_[core] = mm_t(own[:deep], grads[...])
    spread_[1 - core] = mm_t(other[:deep], grads[...])
    flipped = jnp.transpose(jnp.concatenate([hidden[...], jnp.zeros((half, width), F32)]))
    hid[core] = flipped[:ch]
    hid[1 - core] = flipped[ch:]
    granule, count = 24, 16
    for k in range(width // granule):
        block = hid[k % 2, (k // 2) * granule : (k // 2 + 1) * granule, :]
        for tap in range(3):
            row = tap * width + k * granule
            z, c, y = row // 144, (row % 144) // 72, (row % 72) // granule
            at = (y * count + z) * granule
            block = block + spread_[c, at : at + granule, tap * pos : (tap + 1) * pos]
        total[k * granule : (k + 1) * granule, :] = block
    out[...] = jnp.transpose(total[...])[:half]


def rows_of(first, second):
    pos = first.shape[0]
    lane = lax.broadcasted_iota(jnp.int32, (pos, pos), 1)
    return jnp.transpose(jnp.where(lane == 0, first, second))[:2]


def teacher_kernel(member, teacher, member_bias, assay, assay_temp, exp_ref, stats_ref):
    bias = member_bias[pl.ds(member[0], 1), :]
    groups = assay[...][None, :]
    temps = jnp.zeros(groups.shape, F32)
    for k in range(assay_temp.shape[1]):
        temps = jnp.where(groups == k, assay_temp[:, k : k + 1], temps)
    target = (teacher[...].astype(F32) + bias) / temps
    peak = jnp.max(target, axis=1, keepdims=True)
    exps = jnp.exp(target - peak)
    exp_ref[...] = exps
    stats_ref[...] = rows_of(peak, jnp.sum(exps, axis=1, keepdims=True))


def columns_of(rows, count):
    return jnp.transpose(jnp.concatenate([rows, jnp.zeros((count - rows.shape[0], count), F32)]))


def head_kernel(hid_own, hid_other, own, other, target_stats, exp_ref, stats_ref, near_ref):
    near_ref[...] = other[...]
    pos, tracks = exp_ref.shape
    wide = own.shape[2]
    for start in range(0, tracks, wide):
        n = min(wide, tracks - start)
        b = start // wide
        exp_ref[:, start : start + n] = mm(hid_own[...], own[b, :, :n]) + mm(
            hid_other[...], other[b, :, :n]
        )
    peak = jnp.max(exp_ref[...], axis=1, keepdims=True)
    exps = jnp.exp(exp_ref[...] - peak)
    exp_ref[...] = exps
    total = jnp.sum(exps, axis=1, keepdims=True)
    stats_ref[...] = jnp.concatenate([rows_of(peak, total), target_stats[...], jnp.zeros((4, pos), F32)])


def head_back_kernel(yh_ref, exp_s, exp_t, stats, own, other, kept_ref, sent_ref, hg):
    yh = yh_ref[0]
    pos, tracks = exp_s.shape
    wide, ch = own.shape[2], own.shape[1]
    half = pos // 2
    first, second = stats[0], stats[1]
    mine = jnp.where(yh == 0, first, second)

    def scale_of(at):
        top = jnp.maximum(first[at : at + 1], second[at : at + 1])
        total = first[at + 1 : at + 2] * jnp.exp(first[at : at + 1] - top) + second[
            at + 1 : at + 2
        ] * jnp.exp(second[at : at + 1] - top)
        return 2.0 * tracks * jnp.exp(mine[at : at + 1] - top) / total

    scales = columns_of(
        jnp.concatenate([scale_of(0), scale_of(2), jnp.zeros((6, pos), F32)]), pos
    )
    scale_s, scale_t = scales[:, 0:1], scales[:, 1:2]
    grad = (exp_s[...] * scale_s - exp_t[...] * scale_t).astype(BF)
    for source, at in ((own, 0), (other, ch)):
        total = None
        for start in range(0, tracks, wide):
            n = min(wide, tracks - start)
            term = mm_t(grad[:, start : start + n], source[start // wide, :, :n])
            total = term if total is None else total + term
        hg[:, at : at + ch] = total
    kept_ref[...] = hg[pl.ds(pl.multiple_of(yh * half, half), half), :]
    sent_ref[...] = hg[pl.ds(pl.multiple_of((1 - yh) * half, half), half), :].astype(BF)


def back_kernel(yh_ref, kept, received, pre_ref, own, other, grad_ref, hidden_ref):
    yh = yh_ref[0]
    half = kept.shape[0]
    ch = own.shape[1]
    hidden = kept[...] + received[...].astype(F32)
    hidden_ref[...] = hidden
    rounded = hidden.astype(BF)
    deep = own.shape[0] - ch
    gated_grad = mm_t(rounded[:, :ch], own[deep:]) + mm_t(rounded[:, ch:], other[deep:])
    pre = pre_ref[pl.ds(pl.multiple_of(yh * half, half), half), :]
    pre_grad = (gated_grad * gelu_slope(pre)).astype(BF)
    for k in range(grad_ref.shape[0]):
        grad_ref[k] = pre_grad


def on_device(
    inputs, teacher, member, member_bias, assay, assay_temp, conv_weight, proj_weight, head_weight
):
    rows = inputs[0]
    pos, width = rows.shape
    half = pos // 2
    cut, ch = conv_weight.shape
    tracks = head_weight.shape[1]
    zc, cc = lax.axis_size("z"), lax.axis_size(CTX)
    x, yl, core, yh = (lax.axis_index(name) for name in ("x", "yl", "c", "yh"))
    yh_arr = yh.astype(jnp.int32).reshape(1)

    slab = 24
    deep = cut // 2
    deep = cut // 2
    (packed,) = call(
        pack_kernel,
        [SDS((2, slab, ch), BF)],
        [
            pltpu.VMEM(conv_weight.shape, BF),
            pltpu.VMEM(proj_weight.shape, BF),
            pltpu.VMEM(head_weight.shape, BF),
            pltpu.VMEM((cut, ch), F32),
            pltpu.VMEM((2 * slab, 4 * ch), F32),
            pltpu.SemaphoreType.DMA((3,)),
        ],
        2 * slab * width * ch,
        512 * 1024,
        None,
        conv_weight,
        proj_weight,
        head_weight,
        far=(0, 1, 2),
        limit=56,
    )
    gathered = lax.all_gather(packed, "z", axis=0)
    (conv_copies,) = call(
        copies_kernel, [SDS((4, zc, slab, ch), BF)], [], 1024, 1536 * 1024, None, gathered
    )
    over_y = lax.all_to_all(conv_copies, YR, 0, 0).reshape(4 * zc * slab, ch)
    rows_before = shifted(rows, 1)
    rows_after = shifted(rows, -1)
    exp_t, target_stats = call(
        teacher_kernel,
        [SDS((pos, tracks), F32), SDS((2, pos), F32)],
        [],
        4 * pos * tracks,
        1536 * 1024,
        member.astype(jnp.int32),
        teacher[0],
        member_bias,
        assay,
        assay_temp.reshape(1, assay_temp.shape[0]),
        limit=56,
    )
    own = over_y
    other = swapped(own, "c")

    part = cut // cc
    core_arr = core.astype(jnp.int32).reshape(1)
    taps, kinds, by_owner, head_copies = call(
        prepare_kernel,
        [
            SDS((2, pos, zc * deep), BF),
            SDS((2, pos, ch), BF),
            SDS((cc, zc * part, pos), BF),
            SDS((4, zc, slab, ch), BF),
        ],
        [
            pltpu.VMEM((3 * width, pos), F32),
            pltpu.VMEM((2, zc * deep, pos), F32),
            pltpu.VMEM((2, ch, pos), F32),
            pltpu.VMEM((cc, zc * part, pos), F32),
            pltpu.VMEM((2, pos, zc * deep), BF),
            pltpu.VMEM((2, pos, ch), BF),
            pltpu.VMEM((cc, zc * part, pos), BF),
            pltpu.SemaphoreType.DMA((7,)),
        ],
        2 * pos * pos * 3 * width,
        2 * 1024 * 1024,
        core_arr,
        rows_before,
        rows,
        rows_after,
        gathered,
        target_stats,
        far_out=(0, 1, 2, 3),
        limit=56,
    )
    head_own = lax.all_to_all(head_copies, "x", 0, 0).reshape(4, zc * slab, ch)
    pre_act, gated = call(
        conv_kernel,
        [SDS((pos, ch), F32), SDS((pos, ch), BF)],
        [],
        2 * pos * ch * 3 * width,
        3 * 1024 * 1024,
        None,
        taps,
        own,
        other,
    )
    hid_own, hid_other = call(
        hidden_kernel,
        [SDS((pos, ch), BF), SDS((pos, ch), BF)],
        [],
        2 * pos * ch * width,
        1024 * 1024,
        None,
        gated,
        kinds,
        own,
        other,
    )
    head_other = swapped(head_own, "c")

    owned = lax.all_to_all(by_owner, CTX, 0, 0)
    (owned,) = call(
        owned_kernel,
        [SDS((zc * part, cc * half), BF)],
        [],
        1024 * 1024,
        1024 * 1024,
        yh_arr,
        owned,
    )

    exp_s, stats, head_near = call(
        head_kernel,
        [SDS((pos, tracks), F32), SDS((8, pos), F32), SDS(head_other.shape, BF)],
        [],
        2 * pos * width * tracks,
        4 * 1024 * 1024,
        None,
        hid_own,
        hid_other,
        head_own,
        head_other,
        target_stats,
    )
    stats = lax.all_gather(stats, "yh", axis=0)
    kept, sent = call(
        head_back_kernel,
        [SDS((half, width), F32), SDS((half, width), BF)],
        [pltpu.VMEM((pos, width), F32)],
        2 * pos * width * tracks,
        4 * 1024 * 1024,
        yh_arr,
        exp_s,
        exp_t,
        stats,
        head_own,
        head_near,
    )
    received = swapped(sent, "yh")
    copies, hidden_grad = call(
        back_kernel,
        [SDS((cc // 2, half, ch), BF), SDS((half, width), F32)],
        [],
        2 * half * width * ch,
        2 * 1024 * 1024,
        yh_arr,
        kept,
        received,
        pre_act,
        own,
        other,
    )

    by_chip = lax.all_to_all(copies, ("x", "yl"), 0, 0)
    everyone = lax.all_gather(by_chip.reshape(cc // 2 * half, ch), "c", axis=0, tiled=True)
    padded = 16
    (kernel_part,) = call(
        kernel_grad_kernel,
        [SDS((zc, padded, ch), BF)],
        [pltpu.VMEM((zc * part, ch), F32), pltpu.VMEM((zc, padded, ch), F32)],
        2 * zc * part * cc * half * ch,
        2 * 1024 * 1024,
        None,
        owned,
        everyone,
    )
    terms = lax.all_to_all(kernel_part, "z", 0, 0)
    kernel_sum = jnp.sum(terms.astype(F32), axis=0)[:part]
    kernel_pair = lax.all_gather(kernel_sum, "yh", axis=0)
    grad_conv = (kernel_pair[0] + kernel_pair[1]) / math.sqrt(zc * cc * pos)

    (grad_rows,) = call(
        input_grad_kernel,
        [SDS((half, width), F32)],
        [
            pltpu.VMEM((3 * pos, ch), BF),
            pltpu.VMEM((2, zc * deep, 3 * pos), F32),
            pltpu.VMEM((2, ch, pos), F32),
            pltpu.VMEM((width, pos), F32),
        ],
        4 * half * width * ch,
        2 * 1024 * 1024,
        jnp.stack([core, x, yl]).astype(jnp.int32),
        by_chip,
        hidden_grad,
        own,
        other,
    )
    grad_other = swapped(grad_rows, "yh")
    grad_input = jnp.where(
        yh == 0,
        jnp.concatenate([grad_rows, grad_other], axis=0),
        jnp.concatenate([grad_other, grad_rows], axis=0),
    )
    return (grad_input[None], grad_conv)


def solution(mesh):
    fine = Mesh(mesh.devices.reshape(16, 4, 2, 2, 2), ("z", "x", "yl", "c", "yh"))
    return jax.shard_map(
        on_device,
        mesh=fine,
        in_specs=(
            P("z", CTX, None),
            P("z", CTX, "yh"),
            P("z"),
            P(None, "yh"),
            P("yh"),
            P(),
            P("z", None),
            P("z", None),
            P("z", "yh"),
        ),
        out_specs=(P("z", CTX, None), P(("z",) + CTX, None)),
        check_vma=False,
    )
```
